32 devices in a mesh: rep: 2 (over x), node: 2 (over core), local: 8 (over z, y).
Axes of the slice: x: 2, y: 2, z: 4, core: 2. Of those that a mesh axis runs over, the one named last changes fastest.
Arguments:
- tokens: bfloat16 [1024, 3584], P(('rep', 'node', 'local')), parts along dimension 0, may hold values from -6 to 6
- expert_ids: int32 [1024, 8], P(('rep', 'node', 'local')), parts along dimension 0, may hold values from 0 to 15, all different within a row; in each aligned block of 32 rows (0 to 31, 32 to 63, ...) at most 32 rows name the same one
- route_weights: bfloat16 [1024, 8], P(('rep', 'node', 'local')), parts along dimension 0, may hold values from 0.099609375 to 1
- w_up: bfloat16 [16, 3584, 1024], P(('node', 'local')), may hold values from -0.09375 to 0.09375
- w_down: bfloat16 [16, 1024, 3584], P(('node', 'local')), may hold values from -0.1875 to 0.1875
Outputs:
- mixed: bfloat16 [1024, 3584], P(('rep', 'node', 'local')), parts along dimension 0
The draws below stay inside these ranges and needn't reach their ends.
There are 2 independent parts, one for each index of `rep`. The reference program is written for one: setup_inputs(seed, part) draws one part's arguments, and reference() takes and returns one part's arrays. A program takes and returns all parts, laid end to end along the dimension named above; an argument that names none is the same for every part. Nothing has to cross between parts.
Inputs may be any that keep to these rules, and one draw needn't show every extreme that they name: `expert_ids`: the 8 experts of a token differ; in each aligned block of 32 rows (the rows of one device) no expert is named by more than 32 rows.
All inputs are finite; a program needn't handle non-finite values.
Results may differ from the reference program's by a relative error of at most 0.0058.
Values may be sent and summed in bfloat16 or wider, within the bound.
No kernel may reach another device: no remote copies, remote signals or barrier semaphores. Data moves between devices by JAX's collectives and lax.ppermute only.
A program may use at most 64 MiB of HBM per device.

```python
import math
import jax
import jax.numpy as jnp
import numpy as np
from jax import lax

D = 3584
FF = 1024
TOP = 8
TOK_DEV = 32
EXPERTS = 16
MOST = 32
TOKENS = 512


def block_levels(key, shape, cuts, least, largest):
    loudness = 1.0
    for position, parts in cuts:
        steps = jax.random.uniform(jax.random.fold_in(jax.random.fold_in(key, 6), position), (parts,), jnp.float32, least / len(cuts), largest / len(cuts))
        loudness = loudness * jnp.repeat(jnp.exp(steps), shape[position] // parts).reshape((-1,) + (1,) * (len(shape) - 1 - position))
    return loudness


def shared_out(own_key, own, number, rows, amount, top, most, slope):
    order = jax.random.permutation(own_key, amount)
    packed, common = portions_of(amount, rows * top, most, slope, True), portions_of(amount, rows * top, most, slope, False)
    places = jnp.arange(amount)

    def named(tallies, rotation):
        used = int((tallies > 0).sum())
        fixed = max(1, used // 4)
        passed = fixed + (places - fixed + rotation * (used - fixed)) % max(1, amount - fixed)
        return jnp.zeros((amount,), jnp.int32).at[order[jnp.where(places < fixed, places, passed)]].set(jnp.asarray(tallies, jnp.int32))

    tallies = jnp.where(number % 4 == 0, named(packed, number // 4), named(common, number - number // 4 - 1))
    mixed = jax.random.permutation(jax.random.fold_in(own, 3), amount)
    donor, sink = mixed[0:amount // 2 * 2:2], mixed[1:amount // 2 * 2:2]
    slack = jnp.minimum(tallies[donor] - 1, most - tallies[sink]) // 2
    slack = jnp.where((donor == order[0]) | (sink == order[0]) | (tallies[sink] == 0), 0, jnp.maximum(slack, 0))
    passed = jax.random.randint(jax.random.fold_in(own, 4), (amount // 2,), 0, 1 << 20) % (slack + 1)
    tallies = tallies.at[donor].add(-passed).at[sink].add(passed)
    labels = jnp.searchsorted(jnp.cumsum(tallies), jnp.arange(rows * top), side="right").astype(jnp.int32)
    grid = labels.reshape(top, rows).T
    grid = grid[jax.random.permutation(jax.random.fold_in(own, 1), rows)]
    rotation = jax.random.randint(jax.random.fold_in(own, 2), (rows, 1), 0, top)
    return jnp.take_along_axis(grid, (jnp.arange(top)[None, :] + rotation) % top, axis=1)


def portions_of(number_of, total, reach, skew, full):
    portions = [(1 << 20) // math.isqrt(grade ** skew) + 1 for grade in range(1, number_of + 1)]
    largest = reach if full else min(reach, max(-(-total // number_of), total * portions[0] // sum(portions)))
    least = 1 if total - largest >= number_of - 1 else 0
    holding, rest = [largest] + [least] * (number_of - 1), total - largest - least * (number_of - 1)
    while rest > 0:
        candidates = [i for i in range(1, number_of) if holding[i] < largest] or [i for i in range(1, number_of) if holding[i] < reach]
        pool, remaining = sum([portions[i] for i in candidates]), rest
        for i in candidates:
            extra = min(reach - holding[i], max(1, remaining * portions[i] // pool), rest)
            holding[i] = holding[i] + extra
            rest = rest - extra
    return np.array(holding)


def bell_draw(own_key, shape, scale, most, split=(), kind=jnp.bfloat16):
    values = scale * jax.random.normal(own_key, shape, jnp.float32)
    if split:
        values = values * block_levels(own_key, shape, split, -0.22, 0.18)
    return jnp.clip(values, -most, most).astype(kind)


def setup_inputs(seed: int = 0, part: int = 0) -> dict:
    keys = jax.random.split(jax.random.key(seed), 6)
    own_keys = jax.random.split(jax.random.fold_in(keys[5], part), 6)
    tokens = bell_draw(own_keys[0], (TOKENS, D), 1.0, 6.0, ((0, 16),))
    expert_ids_keys = jax.random.split(jax.random.fold_in(own_keys[1], 1), TOKENS // TOK_DEV)
    expert_ids_turns = jax.random.permutation(jax.random.fold_in(own_keys[1], 3), TOKENS // TOK_DEV)
    expert_ids = jax.vmap(lambda own, number: shared_out(jax.random.fold_in(own_keys[1], 2), own, number, TOK_DEV, EXPERTS, TOP, MOST, 2))(expert_ids_keys, expert_ids_turns).reshape((TOKENS, TOP))
    route_weights = jnp.clip(0.099609375 + 0.9003906 * jax.random.uniform(own_keys[2], (TOKENS, TOP), jnp.float32) ** block_levels(own_keys[2], (TOKENS, TOP), ((0, 16),), -0.2, 0.2), 0.099609375, 1.0).astype(jnp.bfloat16)
    w_up = bell_draw(keys[3], (EXPERTS, D, FF), D ** -0.5, 0.09375, ((0, 16),))
    w_down = bell_draw(keys[4], (EXPERTS, FF, D), FF ** -0.5, 0.1875, ((0, 16),))
    return dict(tokens=tokens, expert_ids=expert_ids, route_weights=route_weights, w_up=w_up, w_down=w_down)


def reference(tokens, expert_ids, route_weights, w_up, w_down):
    total = tokens.shape[0]
    top = expert_ids.shape[1]
    flat_ids = expert_ids.reshape(-1)
    flat_weights = route_weights.reshape(-1).astype(jnp.float32)
    bound = EXPERTS * MOST
    filler = total * top

    def one_expert(carry, inputs):
        index, up, down = inputs
        picks = jnp.nonzero(flat_ids == index, size=bound, fill_value=filler)[0].astype(jnp.int32)
        valid = picks < filler
        token_rows = jnp.where(valid, picks // top, 0).astype(jnp.int32)
        rows = tokens[token_rows]
        hidden = jax.nn.silu(jnp.dot(rows, up, preferred_element_type=jnp.float32)).astype(jnp.bfloat16)
        answer = jnp.dot(hidden, down, preferred_element_type=jnp.float32).astype(jnp.bfloat16)
        scale = jnp.where(valid, flat_weights[jnp.minimum(picks, filler - 1)], 0.0)
        return carry.at[token_rows].add(scale[:, None] * answer.astype(jnp.float32)), None

    start = jnp.zeros((total, tokens.shape[1]), jnp.float32)
    result, _ = lax.scan(one_expert, start, (jnp.arange(EXPERTS, dtype=jnp.int32), w_up, w_down))
    return result.astype(jnp.bfloat16)
```

```python
import jax
import jax.numpy as jnp
from jax import lax
from jax.sharding import PartitionSpec as P


def per_device(tokens, expert_ids, route_weights, w_up, w_down):
    axes = ("node", "local")
    mine = lax.axis_index(axes)
    everyone = lax.all_gather(tokens, axes, tiled=True)
    ids = lax.all_gather(expert_ids, axes, tiled=True)
    weights = lax.all_gather(route_weights, axes, tiled=True)
    scale = jnp.sum(jnp.where(ids == mine, weights.astype(jnp.float32), 0.0), axis=1)
    hidden = jax.nn.silu(jnp.dot(everyone, w_up[0], preferred_element_type=jnp.float32)).astype(jnp.bfloat16)
    answer = jnp.dot(hidden, w_down[0], preferred_element_type=jnp.float32)
    part = (answer * scale[:, None]).astype(jnp.bfloat16)
    return lax.psum_scatter(part, axes, scatter_dimension=0, tiled=True)


def solution(mesh):
    placed = (
        P(("rep", "node", "local"), None),
        P(("rep", "node", "local"), None),
        P(("rep", "node", "local"), None),
        P(("node", "local"), None, None),
        P(("node", "local"), None, None),
    )
    return jax.shard_map(
        per_device,
        mesh=mesh,
        in_specs=placed,
        out_specs=P(("rep", "node", "local"), None),
        check_vma=False,
    )
```

```python
import jax
import jax.numpy as jnp
from jax import lax
from jax.sharding import PartitionSpec as P

BOTH = ("node", "local")
LANES = 128


def gather_plan(tokens, expert_ids, route_weights, w_up, w_down):
    mine = lax.axis_index(BOTH)
    everyone = lax.all_gather(tokens, BOTH, tiled=True)
    ids = lax.all_gather(expert_ids, BOTH, tiled=True)
    weights = lax.all_gather(route_weights, BOTH, tiled=True)
    scale = jnp.sum(jnp.where(ids == mine, weights.astype(jnp.float32), 0.0), axis=1)
    hidden = jax.nn.silu(jnp.dot(everyone, w_up[0], preferred_element_type=jnp.float32)).astype(jnp.bfloat16)
    answer = jnp.dot(hidden, w_down[0], preferred_element_type=jnp.float32)
    part = (answer * scale[:, None]).astype(jnp.bfloat16)
    return lax.psum_scatter(part, BOTH, scatter_dimension=0, tiled=True)


def ring_plan(tokens, expert_ids, route_weights, w_up, w_down):
    rows, width = tokens.shape
    experts = lax.axis_size(BOTH)
    n = lax.axis_size("local")
    half = n // 2
    mine = lax.axis_index(BOTH)
    order = list(range(0, n, 2)) + list(range(n - 1, 0, -2))
    onward = [(order[i], order[(i + 1) % n]) for i in range(n)]
    pairs = onward + [(n + b, n + a) for a, b in onward]

    def hop(x):
        return lax.ppermute(x, BOTH, pairs)

    def swap(x):
        return lax.ppermute(x, "node", [(0, 1), (1, 0)])

    columns = -(-experts // LANES) * LANES
    named = expert_ids[:, :, None] == jnp.arange(columns, dtype=jnp.int32)[None, None, :]
    table = jnp.sum(jnp.where(named, route_weights.astype(jnp.float32)[:, :, None], 0.0), axis=1)
    own = jnp.concatenate([tokens, table.astype(jnp.bfloat16)], axis=1)

    def expert(blocks):
        x = jnp.concatenate(blocks, axis=0)
        here = jnp.arange(columns, dtype=jnp.int32)[None, :] == mine
        scale = jnp.sum(jnp.where(here, x[:, width:].astype(jnp.float32), 0.0), axis=1)
        up = jnp.dot(x[:, :width], w_up[0], preferred_element_type=jnp.float32)
        hidden = jax.nn.silu(up).astype(jnp.bfloat16)
        answer = jnp.dot(hidden, w_down[0], preferred_element_type=jnp.float32)
        answer = answer.astype(jnp.bfloat16).astype(jnp.float32)
        out = answer * scale[:, None]
        return [out[i * rows:(i + 1) * rows] for i in range(len(blocks))]

    a, b = [own], [swap(own)]
    for h in range(1, half):
        a.append(hop(a[-1]))
        b.append(hop(b[-1]))
    a.append(hop(a[-1]))
    ahead_b = [None] + [swap(a[h]) for h in range(1, half + 1)]
    ahead_a = [None] + [swap(b[h]) for h in range(1, half)]

    p_own = expert([a[0], b[0]])
    behind, ahead = {}, {}
    for h in range(1, half):
        r = expert([a[h], b[h], ahead_a[h], ahead_b[h]])
        behind[h] = r[:2]
        ahead[h] = r[2:]
    far = expert([a[half], ahead_b[half]])

    def bf(x):
        return x.astype(jnp.bfloat16)

    got_far = swap(bf(far[1]))
    sums = {half: [far[0] + got_far.astype(jnp.float32)]}
    for h in range(half - 1, 0, -1):
        ga = swap(bf(behind[h][1]))
        gb = swap(bf(behind[h][0]))
        sums[h] = [ahead[h][0] + ga.astype(jnp.float32), ahead[h][1] + gb.astype(jnp.float32)]

    run_b = hop(bf(sums[half - 1][1]))
    run_a = hop(bf(sums[half][0]))
    for h in range(half - 1, 0, -1):
        if h < half - 1:
            run_b = hop(bf(sums[h][1] + run_b.astype(jnp.float32)))
        run_a = hop(bf(sums[h][0] + run_a.astype(jnp.float32)))
    last = swap(bf(p_own[1] + run_b.astype(jnp.float32)))
    return bf(p_own[0] + run_a.astype(jnp.float32) + last.astype(jnp.float32))


def solution(mesh):
    placed = (
        P(("rep", "node", "local"), None),
        P(("rep", "node", "local"), None),
        P(("rep", "node", "local"), None),
        P(("node", "local"), None, None),
        P(("node", "local"), None, None),
    )
    n = mesh.shape["local"]
    ringed = mesh.shape["node"] == 2 and n % 2 == 0 and 4 <= n <= 16
    return jax.shard_map(
        ring_plan if ringed else gather_plan,
        mesh=mesh,
        in_specs=placed,
        out_specs=P(("rep", "node", "local"), None),
        check_vma=False,
    )
```

```python
import functools
import jax
import jax.numpy as jnp
from jax import lax
from jax.experimental import pallas as pl
from jax.experimental.pallas import tpu as pltpu
from jax.sharding import PartitionSpec as P

BOTH = ("node", "local")
LANES = 128


def gather_plan(tokens, expert_ids, route_weights, w_up, w_down):
    mine = lax.axis_index(BOTH)
    everyone = lax.all_gather(tokens, BOTH, tiled=True)
    ids = lax.all_gather(expert_ids, BOTH, tiled=True)
    weights = lax.all_gather(route_weights, BOTH, tiled=True)
    scale = jnp.sum(jnp.where(ids == mine, weights.astype(jnp.float32), 0.0), axis=1)
    hidden = jax.nn.silu(jnp.dot(everyone, w_up[0], preferred_element_type=jnp.float32)).astype(jnp.bfloat16)
    answer = jnp.dot(hidden, w_down[0], preferred_element_type=jnp.float32)
    part = (answer * scale[:, None]).astype(jnp.bfloat16)
    return lax.psum_scatter(part, BOTH, scatter_dimension=0, tiled=True)


def step_of(size, wanted):
    step = wanted
    while step > LANES and size % step:
        step //= 2
    return step if size % step == 0 else size


def expert_body(blocks, kept, mine_ref, *refs):
    tokens = refs[:blocks]
    up_ref, down_ref = refs[blocks:blocks + 2]
    outs = refs[blocks + 2:2 * blocks + 2]
    hidden_ref = refs[2 * blocks + 2]
    width, middle = up_ref.shape
    rows = tokens[0].shape[0]
    x = jnp.concatenate([t[:, :width] for t in tokens], axis=0)
    table = jnp.concatenate([t[:, width:] for t in tokens], axis=0).astype(jnp.float32)
    here = lax.broadcasted_iota(jnp.int32, table.shape, 1) == mine_ref[0]
    scale = jnp.sum(jnp.where(here, table, 0.0), axis=1, keepdims=True)
    step = step_of(middle, 256)
    for j in range(0, middle, step):
        up = jnp.dot(x, up_ref[:, j:j + step], preferred_element_type=jnp.float32)
        hidden_ref[:, j:j + step] = (up / (1.0 + jnp.exp(-up))).astype(jnp.bfloat16)
    hidden = hidden_ref[...]
    step = step_of(width, 512)
    for j in range(0, width, step):
        answer = jnp.dot(hidden, down_ref[:, j:j + step], preferred_element_type=jnp.float32)
        answer = answer.astype(jnp.bfloat16).astype(jnp.float32) * scale
        for i in range(blocks):
            outs[i][:, j:j + step] = answer[i * rows:(i + 1) * rows].astype(outs[i].dtype)


def expert(mine, blocks, kept, up, down):
    rows = blocks[0].shape[0]
    width, middle = up.shape
    total = rows * len(blocks)
    vmem = pl.BlockSpec(memory_space=pltpu.VMEM)
    return pl.pallas_call(
        functools.partial(expert_body, len(blocks), kept),
        out_shape=[
            jax.ShapeDtypeStruct((rows, width), jnp.float32 if k else jnp.bfloat16) for k in kept
        ],
        in_specs=[pl.BlockSpec(memory_space=pltpu.SMEM)] + [vmem] * (len(blocks) + 2),
        out_specs=[vmem] * len(blocks),
        scratch_shapes=[pltpu.VMEM((total, middle), jnp.bfloat16)],
        compiler_params=pltpu.CompilerParams(vmem_limit_bytes=24 * 2**20),
        cost_estimate=pl.CostEstimate(
            flops=4 * total * width * middle, bytes_accessed=4 * width * middle, transcendentals=total * middle
        ),
    )(mine, *blocks, up, down)


def first_body(mine_ref, own_ref, other_ref, up_hbm, down_hbm, out_own, out_other, up_ref, down_ref, hidden_ref, sems):
    width, middle = up_ref.shape
    up_step, down_step = step_of(middle, 256), step_of(width, 512)
    copies = []
    for j in range(0, middle, up_step):
        s = pl.ds(j, up_step)
        copies.append(pltpu.make_async_copy(up_hbm.at[:, s], up_ref.at[:, s], sems.at[len(copies)]))
    for j in range(0, width, down_step):
        s = pl.ds(j, down_step)
        copies.append(pltpu.make_async_copy(down_hbm.at[:, s], down_ref.at[:, s], sems.at[len(copies)]))
    for c in copies:
        c.start()
    rows = own_ref.shape[0]
    x = jnp.concatenate([own_ref[:, :width], other_ref[:, :width]], axis=0)
    table = jnp.concatenate([own_ref[:, width:], other_ref[:, width:]], axis=0).astype(jnp.float32)
    here = lax.broadcasted_iota(jnp.int32, table.shape, 1) == mine_ref[0]
    scale = jnp.sum(jnp.where(here, table, 0.0), axis=1, keepdims=True)
    for j in range(0, middle, up_step):
        copies[j // up_step].wait()
        up = jnp.dot(x, up_ref[:, j:j + up_step], preferred_element_type=jnp.float32)
        hidden_ref[:, j:j + up_step] = (up / (1.0 + jnp.exp(-up))).astype(jnp.bfloat16)
    hidden = hidden_ref[...]
    for j in range(0, width, down_step):
        copies[middle // up_step + j // down_step].wait()
        answer = jnp.dot(hidden, down_ref[:, j:j + down_step], preferred_element_type=jnp.float32)
        answer = answer.astype(jnp.bfloat16).astype(jnp.float32) * scale
        out_own[:, j:j + down_step] = answer[:rows]
        out_other[:, j:j + down_step] = answer[rows:]


def first_expert(mine, own, other, w_up, w_down):
    rows = own.shape[0]
    width, middle = w_up.shape
    chunks = middle // step_of(middle, 256) + width // step_of(width, 512)
    vmem, anywhere = pl.BlockSpec(memory_space=pltpu.VMEM), pl.BlockSpec(memory_space=pl.ANY)
    return pl.pallas_call(
        first_body,
        out_shape=[jax.ShapeDtypeStruct((rows, width), jnp.float32)] * 2
        + [pltpu.VMEM(w_up.shape, w_up.dtype), pltpu.VMEM(w_down.shape, w_down.dtype)],
        in_specs=[pl.BlockSpec(memory_space=pltpu.SMEM), vmem, vmem, anywhere, anywhere],
        out_specs=[vmem] * 4,
        scratch_shapes=[pltpu.VMEM((2 * rows, middle), jnp.bfloat16), pltpu.SemaphoreType.DMA((chunks,))],
        compiler_params=pltpu.CompilerParams(vmem_limit_bytes=32 * 2**20),
        cost_estimate=pl.CostEstimate(
            flops=8 * rows * width * middle, bytes_accessed=4 * width * middle, transcendentals=2 * rows * middle
        ),
    )(mine, own, other, w_up, w_down)


def label_body(tokens_ref, ids_ref, weights_ref, out_ref):
    rows, width = tokens_ref.shape
    out_ref[:, :width] = tokens_ref[...]
    columns = out_ref.shape[1] - width
    column = lax.broadcasted_iota(jnp.int32, (rows, columns), 1)
    weights = weights_ref[...].astype(jnp.float32)
    table = jnp.zeros((rows, columns), jnp.float32)
    for k in range(ids_ref.shape[1]):
        table = jnp.where(ids_ref[:, k:k + 1] == column, weights[:, k:k + 1], table)
    out_ref[:, width:] = table.astype(jnp.bfloat16)


def label(tokens, expert_ids, route_weights, columns):
    rows, width = tokens.shape
    vmem = pl.BlockSpec(memory_space=pltpu.VMEM)
    return pl.pallas_call(
        label_body,
        out_shape=jax.ShapeDtypeStruct((rows, width + columns), jnp.bfloat16),
        in_specs=[vmem] * 3,
        out_specs=vmem,
    )(tokens, expert_ids, route_weights)


def ring_plan(tokens, expert_ids, route_weights, w_up, w_down):
    rows, width = tokens.shape
    experts = lax.axis_size(BOTH)
    n = lax.axis_size("local")
    half = n // 2
    mine = lax.axis_index(BOTH).astype(jnp.int32)[None]
    order = list(range(0, n, 2)) + list(range(n - 1, 0, -2))
    onward = [(order[i], order[(i + 1) % n]) for i in range(n)]
    pairs = onward + [(n + b, n + a) for a, b in onward]
    def hop(x):
        return lax.ppermute(x, BOTH, pairs)

    def swap(x):
        return lax.ppermute(x, "node", [(0, 1), (1, 0)])

    def bf(x):
        return x.astype(jnp.bfloat16)

    columns = -(-experts // LANES) * LANES
    own = label(tokens, expert_ids, route_weights, columns)

    a, b = [own], [swap(own)]
    own_a, own_b, up, down = first_expert(mine, own, b[0], w_up[0], w_down[0])
    ahead_a, ahead_b = [None], [None]
    behind, ahead = {}, {}
    for h in range(1, half):
        a.append(hop(a[-1]))
        b.append(hop(b[-1]))
        if h == 1:
            up, down, b[1] = lax.optimization_barrier((up, down, b[1]))
            up = pltpu.with_memory_space_constraint(up, pltpu.VMEM)
            down = pltpu.with_memory_space_constraint(down, pltpu.VMEM)
        ahead_b.append(swap(a[h]))
        ahead_a.append(swap(b[h]))
        if h >= 2:
            done = (a[h - 1], b[h - 1], ahead_a[h - 1], ahead_b[h - 1])
            r = expert(mine, done, (False, False, True, True), up, down)
            behind[h - 1], ahead[h - 1] = r[:2], r[2:]
            a[h], behind[h - 1], ahead[h - 1] = lax.optimization_barrier((a[h], behind[h - 1], ahead[h - 1]))
    a.append(hop(a[-1]))
    ahead_b.append(swap(a[half]))
    h = half - 1
    r = expert(mine, (a[h], b[h], ahead_a[h], ahead_b[h]), (False, False, True, True), up, down)
    behind[h], ahead[h] = r[:2], r[2:]
    far = expert(mine, (a[half], ahead_b[half]), (True, False), up, down)

    sums = {half: [far[0] + swap(far[1]).astype(jnp.float32)]}
    for h in range(half - 1, 0, -1):
        sums[h] = [
            ahead[h][0] + swap(behind[h][1]).astype(jnp.float32),
            ahead[h][1] + swap(behind[h][0]).astype(jnp.float32),
        ]
    run_b = hop(bf(sums[half - 1][1]))
    run_a = hop(bf(sums[half][0]))
    for h in range(half - 1, 0, -1):
        if h < half - 1:
            run_b = hop(bf(sums[h][1] + run_b.astype(jnp.float32)))
        run_a = hop(bf(sums[h][0] + run_a.astype(jnp.float32)))
    last = swap(bf(own_b + run_b.astype(jnp.float32)))
    return bf(own_a + run_a.astype(jnp.float32) + last.astype(jnp.float32))


def solution(mesh):
    placed = (
        P(("rep", "node", "local"), None),
        P(("rep", "node", "local"), None),
        P(("rep", "node", "local"), None),
        P(("node", "local"), None, None),
        P(("node", "local"), None, None),
    )
    n = mesh.shape["local"]
    ringed = mesh.shape["node"] == 2 and n % 2 == 0 and 4 <= n <= 16
    return jax.shard_map(
        ring_plan if ringed else gather_plan,
        mesh=mesh,
        in_specs=placed,
        out_specs=P(("rep", "node", "local"), None),
        check_vma=False,
    )
```

```python
import functools
import jax
import jax.numpy as jnp
from jax import lax
from jax.experimental import pallas as pl
from jax.experimental.pallas import tpu as pltpu
from jax.sharding import PartitionSpec as P

BOTH = ("node", "local")
LANES = 128


def gather_plan(tokens, expert_ids, route_weights, w_up, w_down):
    mine = lax.axis_index(BOTH)
    everyone = lax.all_gather(tokens, BOTH, tiled=True)
    ids = lax.all_gather(expert_ids, BOTH, tiled=True)
    weights = lax.all_gather(route_weights, BOTH, tiled=True)
    scale = jnp.sum(jnp.where(ids == mine, weights.astype(jnp.float32), 0.0), axis=1)
    hidden = jax.nn.silu(jnp.dot(everyone, w_up[0], preferred_element_type=jnp.float32)).astype(jnp.bfloat16)
    answer = jnp.dot(hidden, w_down[0], preferred_element_type=jnp.float32)
    part = (answer * scale[:, None]).astype(jnp.bfloat16)
    return lax.psum_scatter(part, BOTH, scatter_dimension=0, tiled=True)


def step_of(size, wanted):
    step = wanted
    while step > LANES and size % step:
        step //= 2
    return step if size % step == 0 else size


def expert_body(blocks, kept, mine_ref, *refs):
    tokens = refs[:blocks]
    up_ref, down_ref = refs[blocks:blocks + 2]
    outs = refs[blocks + 2:2 * blocks + 2]
    hidden_ref = refs[2 * blocks + 2]
    width, middle = up_ref.shape
    rows = tokens[0].shape[0]
    x = jnp.concatenate([t[:, :width] for t in tokens], axis=0)
    table = jnp.concatenate([t[:, width:] for t in tokens], axis=0).astype(jnp.float32)
    here = lax.broadcasted_iota(jnp.int32, table.shape, 1) == mine_ref[0]
    scale = jnp.sum(jnp.where(here, table, 0.0), axis=1, keepdims=True)
    step = step_of(middle, 256)
    for j in range(0, middle, step):
        up = jnp.dot(x, up_ref[:, j:j + step], preferred_element_type=jnp.float32)
        hidden_ref[:, j:j + step] = (up / (1.0 + jnp.exp(-up))).astype(jnp.bfloat16)
    hidden = hidden_ref[...]
    step = step_of(width, 512)
    for j in range(0, width, step):
        answer = jnp.dot(hidden, down_ref[:, j:j + step], preferred_element_type=jnp.float32)
        answer = answer.astype(jnp.bfloat16).astype(jnp.float32) * scale
        for i in range(blocks):
            outs[i][:, j:j + step] = answer[i * rows:(i + 1) * rows].astype(outs[i].dtype)


def expert(mine, blocks, kept, up, down):
    rows = blocks[0].shape[0]
    width, middle = up.shape
    total = rows * len(blocks)
    vmem = pl.BlockSpec(memory_space=pltpu.VMEM)
    return pl.pallas_call(
        functools.partial(expert_body, len(blocks), kept),
        out_shape=[
            jax.ShapeDtypeStruct((rows, width), jnp.float32 if k else jnp.bfloat16) for k in kept
        ],
        in_specs=[pl.BlockSpec(memory_space=pltpu.SMEM)] + [vmem] * (len(blocks) + 2),
        out_specs=[vmem] * len(blocks),
        scratch_shapes=[pltpu.VMEM((total, middle), jnp.bfloat16)],
        compiler_params=pltpu.CompilerParams(vmem_limit_bytes=16 * 2**20),
        cost_estimate=pl.CostEstimate(
            flops=4 * total * width * middle, bytes_accessed=4 * width * middle, transcendentals=total * middle
        ),
    )(mine, *blocks, up, down)


def first_up_body(mine_ref, own_ref, other_ref, up_hbm, hidden_ref, scale_ref, up_ref, sems):
    width, middle = up_ref.shape
    step = step_of(middle, 256)
    copies = []
    for j in range(0, middle, step):
        s = pl.ds(j, step)
        copies.append(pltpu.make_async_copy(up_hbm.at[:, s], up_ref.at[:, s], sems.at[len(copies)]))
        copies[-1].start()
    x = jnp.concatenate([own_ref[:, :width], other_ref[:, :width]], axis=0)
    table = jnp.concatenate([own_ref[:, width:], other_ref[:, width:]], axis=0).astype(jnp.float32)
    here = lax.broadcasted_iota(jnp.int32, table.shape, 1) == mine_ref[0]
    scale_ref[...] = jnp.broadcast_to(jnp.sum(jnp.where(here, table, 0.0), axis=1, keepdims=True), scale_ref.shape)
    for j in range(0, middle, step):
        copies[j // step].wait()
        up = jnp.dot(x, up_ref[:, j:j + step], preferred_element_type=jnp.float32)
        hidden_ref[:, j:j + step] = (up / (1.0 + jnp.exp(-up))).astype(jnp.bfloat16)


def first_up(mine, own, other, w_up):
    rows = own.shape[0]
    width, middle = w_up.shape
    vmem, hbm = pl.BlockSpec(memory_space=pltpu.VMEM), pl.BlockSpec(memory_space=pltpu.HBM)
    return pl.pallas_call(
        first_up_body,
        out_shape=[
            pltpu.VMEM((2 * rows, middle), jnp.bfloat16),
            pltpu.VMEM((2 * rows, LANES), jnp.float32),
            pltpu.VMEM(w_up.shape, w_up.dtype),
        ],
        in_specs=[pl.BlockSpec(memory_space=pltpu.SMEM), vmem, vmem, hbm],
        out_specs=[vmem] * 3,
        scratch_shapes=[pltpu.SemaphoreType.DMA((middle // step_of(middle, 256),))],
        compiler_params=pltpu.CompilerParams(vmem_limit_bytes=16 * 2**20),
        cost_estimate=pl.CostEstimate(
            flops=4 * rows * width * middle, bytes_accessed=2 * width * middle, transcendentals=2 * rows * middle
        ),
    )(mine, own, other, pltpu.with_memory_space_constraint(w_up, pltpu.HBM))


def first_down_body(hidden_ref, scale_ref, down_hbm, out_own, out_other, down_ref, sems):
    middle, width = down_ref.shape
    step = step_of(width, 512)
    copies = []
    for j in range(0, width, step):
        s = pl.ds(j, step)
        copies.append(pltpu.make_async_copy(down_hbm.at[:, s], down_ref.at[:, s], sems.at[len(copies)]))
        copies[-1].start()
    rows = out_own.shape[0]
    scale = scale_ref[:, :1]
    hidden = hidden_ref[...]
    for j in range(0, width, step):
        copies[j // step].wait()
        answer = jnp.dot(hidden, down_ref[:, j:j + step], preferred_element_type=jnp.float32)
        answer = answer.astype(jnp.bfloat16).astype(jnp.float32) * scale
        out_own[:, j:j + step] = answer[:rows]
        out_other[:, j:j + step] = answer[rows:]


def first_down(hidden, scale, w_down):
    rows = hidden.shape[0] // 2
    middle, width = w_down.shape
    vmem, hbm = pl.BlockSpec(memory_space=pltpu.VMEM), pl.BlockSpec(memory_space=pltpu.HBM)
    return pl.pallas_call(
        first_down_body,
        out_shape=[pltpu.VMEM((rows, width), jnp.float32)] * 2 + [pltpu.VMEM(w_down.shape, w_down.dtype)],
        in_specs=[vmem, vmem, hbm],
        out_specs=[vmem] * 3,
        scratch_shapes=[pltpu.SemaphoreType.DMA((width // step_of(width, 512),))],
        compiler_params=pltpu.CompilerParams(vmem_limit_bytes=16 * 2**20),
        cost_estimate=pl.CostEstimate(
            flops=4 * rows * width * middle, bytes_accessed=2 * width * middle, transcendentals=0
        ),
    )(hidden, scale, pltpu.with_memory_space_constraint(w_down, pltpu.HBM))


def label_body(tokens_ref, ids_ref, weights_ref, out_ref):
    rows, width = tokens_ref.shape
    columns = out_ref.shape[1] - width
    expert_of = lax.broadcasted_iota(jnp.int32, (columns, rows), 0)
    weights = weights_ref[...].astype(jnp.float32)
    table = jnp.zeros((columns, rows), jnp.float32)
    for k in range(ids_ref.shape[0]):
        table = jnp.where(ids_ref[k:k + 1, :] == expert_of, weights[k:k + 1, :], table)
    one = lax.broadcasted_iota(jnp.int32, (rows, rows), 0) == lax.broadcasted_iota(jnp.int32, (rows, rows), 1)
    turned = lax.dot_general(
        one.astype(jnp.bfloat16),
        table.astype(jnp.bfloat16),
        (((1,), (1,)), ((), ())),
        preferred_element_type=jnp.float32,
    )
    out_ref[:, :width] = tokens_ref[...]
    out_ref[:, width:] = turned.astype(jnp.bfloat16)


def label(tokens, expert_ids, route_weights, columns):
    rows, width = tokens.shape
    vmem = pl.BlockSpec(memory_space=pltpu.VMEM)
    return pl.pallas_call(
        label_body,
        out_shape=pltpu.VMEM((rows, width + columns), jnp.bfloat16),
        in_specs=[vmem] * 3,
        out_specs=vmem,
    )(tokens, expert_ids.T, route_weights.T)


def ring_plan(tokens, expert_ids, route_weights, w_up, w_down):
    rows, width = tokens.shape
    experts = lax.axis_size(BOTH)
    n = lax.axis_size("local")
    half = n // 2
    mine = lax.axis_index(BOTH).astype(jnp.int32)[None]
    order = list(range(0, n, 2)) + list(range(n - 1, 0, -2))
    onward = [(order[i], order[(i + 1) % n]) for i in range(n)]
    pairs = onward + [(n + b, n + a) for a, b in onward]
    def hop(x):
        return lax.ppermute(x, BOTH, pairs)

    def swap(x):
        return lax.ppermute(x, "node", [(0, 1), (1, 0)])

    def bf(x):
        return x.astype(jnp.bfloat16)

    columns = -(-experts // LANES) * LANES
    own = label(tokens, expert_ids, route_weights, columns)

    a, b = [own], [swap(own)]
    ahead_a, ahead_b = [None], [None]
    behind, ahead = {}, {}

    def compute(h, first=None):
        blocks = (a[h], b[h], ahead_a[h], ahead_b[h])
        if first is not None:
            blocks, _ = lax.optimization_barrier((blocks, first))
        r = expert(mine, blocks, (False, False, True, True), up, down)
        behind[h], ahead[h] = r[:2], r[2:]

    hidden, scale, up = first_up(mine, own, b[0], w_up[0])
    for h in range(1, half + 1):
        a.append(hop(a[-1]))
        if h < half:
            b.append(hop(b[-1]))
        if h == 1:
            a[1], hidden, up = lax.optimization_barrier((a[1], hidden, up))
            up = pltpu.with_memory_space_constraint(up, pltpu.VMEM)
        elif h == 2:
            own_a, own_b, down = first_down(hidden, scale, w_down[0])
            a[2], own_a, own_b, down = lax.optimization_barrier((a[2], own_a, own_b, down))
            down = pltpu.with_memory_space_constraint(down, pltpu.VMEM)
        elif h < half:
            compute(h - 2)
            a[h], behind[h - 2], ahead[h - 2] = lax.optimization_barrier((a[h], behind[h - 2], ahead[h - 2]))
        if h < half:
            ahead_b.append(swap(a[h]))
            ahead_a.append(swap(b[h]))
    compute(half - 1, (ahead_a[half - 2], ahead_b[half - 2]))
    a[half], behind[half - 1], ahead[half - 1] = lax.optimization_barrier((a[half], behind[half - 1], ahead[half - 1]))
    ahead_b.append(swap(a[half]))

    def join(x, y):
        return x.astype(jnp.float32) + y.astype(jnp.float32)

    def total(h):
        return [join(ahead[h][0], swap(behind[h][1])), join(ahead[h][1], swap(behind[h][0]))]

    sums = total(half - 1)
    send_b = bf(sums[1])
    run_b = hop(send_b)
    last_blocks, send_b = lax.optimization_barrier(((a[half], ahead_b[half]), send_b))
    far = expert(mine, last_blocks, (True, False), up, down)
    send_a = bf(join(far[0], swap(far[1])))
    run_a = hop(send_a)
    for h in range(half - 1, 0, -1):
        if h < half - 1:
            if h not in behind:
                compute(h, far)
            sums = total(h)
            run_b = hop(bf(join(sums[1], run_b)))
        run_a = hop(bf(join(sums[0], run_a)))
    last = swap(bf(join(own_b, run_b)))
    return bf(join(join(own_a, run_a), last))


def solution(mesh):
    placed = (
        P(("rep", "node", "local"), None),
        P(("rep", "node", "local"), None),
        P(("rep", "node", "local"), None),
        P(("node", "local"), None, None),
        P(("node", "local"), None, None),
    )
    n = mesh.shape["local"]
    ringed = mesh.shape["node"] == 2 and n % 2 == 0 and 4 <= n <= 16
    return jax.shard_map(
        ring_plan if ringed else gather_plan,
        mesh=mesh,
        in_specs=placed,
        out_specs=P(("rep", "node", "local"), None),
        check_vma=False,
    )
```

```python
import functools
import jax
import jax.numpy as jnp
from jax import lax
from jax.experimental import pallas as pl
from jax.experimental.pallas import tpu as pltpu
from jax.sharding import PartitionSpec as P

BOTH = ("node", "local")
LANES = 128


def gather_plan(tokens, expert_ids, route_weights, w_up, w_down):
    mine = lax.axis_index(BOTH)
    everyone = lax.all_gather(tokens, BOTH, tiled=True)
    ids = lax.all_gather(expert_ids, BOTH, tiled=True)
    weights = lax.all_gather(route_weights, BOTH, tiled=True)
    scale = jnp.sum(jnp.where(ids == mine, weights.astype(jnp.float32), 0.0), axis=1)
    hidden = jax.nn.silu(jnp.dot(everyone, w_up[0], preferred_element_type=jnp.float32)).astype(jnp.bfloat16)
    answer = jnp.dot(hidden, w_down[0], preferred_element_type=jnp.float32)
    part = (answer * scale[:, None]).astype(jnp.bfloat16)
    return lax.psum_scatter(part, BOTH, scatter_dimension=0, tiled=True)


def step_of(size, wanted):
    step = wanted
    while step > LANES and size % step:
        step //= 2
    return step if size % step == 0 else size


def expert_body(blocks, kept, mine_ref, *refs):
    tokens = refs[:blocks]
    up_ref, down_ref = refs[blocks:blocks + 2]
    outs = refs[blocks + 2:2 * blocks + 2]
    hidden_ref = refs[2 * blocks + 2]
    width, middle = up_ref.shape
    rows = tokens[0].shape[0]
    x = jnp.concatenate([t[:, :width] for t in tokens], axis=0)
    table = jnp.concatenate([t[:, width:] for t in tokens], axis=0).astype(jnp.float32)
    here = lax.broadcasted_iota(jnp.int32, table.shape, 1) == mine_ref[0]
    scale = jnp.sum(jnp.where(here, table, 0.0), axis=1, keepdims=True)
    step = step_of(middle, 256)
    for j in range(0, middle, step):
        up = jnp.dot(x, up_ref[:, j:j + step], preferred_element_type=jnp.float32)
        hidden_ref[:, j:j + step] = (up / (1.0 + jnp.exp(-up))).astype(jnp.bfloat16)
    hidden = hidden_ref[...]
    step = step_of(width, 512)
    for j in range(0, width, step):
        answer = jnp.dot(hidden, down_ref[:, j:j + step], preferred_element_type=jnp.float32)
        answer = answer.astype(jnp.bfloat16).astype(jnp.float32) * scale
        for i in range(blocks):
            outs[i][:, j:j + step] = answer[i * rows:(i + 1) * rows].astype(outs[i].dtype)


def expert(mine, blocks, kept, up, down):
    rows = blocks[0].shape[0]
    width, middle = up.shape
    total = rows * len(blocks)
    vmem = pl.BlockSpec(memory_space=pltpu.VMEM)
    return pl.pallas_call(
        functools.partial(expert_body, len(blocks), kept),
        out_shape=[
            jax.ShapeDtypeStruct((rows, width), jnp.float32 if k else jnp.bfloat16) for k in kept
        ],
        in_specs=[pl.BlockSpec(memory_space=pltpu.SMEM)] + [vmem] * (len(blocks) + 2),
        out_specs=[vmem] * len(blocks),
        scratch_shapes=[pltpu.VMEM((total, middle), jnp.bfloat16)],
        compiler_params=pltpu.CompilerParams(vmem_limit_bytes=16 * 2**20),
        cost_estimate=pl.CostEstimate(
            flops=4 * total * width * middle, bytes_accessed=4 * width * middle, transcendentals=total * middle
        ),
    )(mine, *blocks, up, down)


def first_up_body(mine_ref, own_ref, other_ref, up_hbm, hidden_ref, scale_ref, up_ref, sems):
    width, middle = up_ref.shape
    step = step_of(middle, 256)
    copies = []
    for j in range(0, middle, step):
        s = pl.ds(j, step)
        copies.append(pltpu.make_async_copy(up_hbm.at[:, s], up_ref.at[:, s], sems.at[len(copies)]))
        copies[-1].start()
    x = jnp.concatenate([own_ref[:, :width], other_ref[:, :width]], axis=0)
    table = jnp.concatenate([own_ref[:, width:], other_ref[:, width:]], axis=0).astype(jnp.float32)
    here = lax.broadcasted_iota(jnp.int32, table.shape, 1) == mine_ref[0]
    scale_ref[...] = jnp.broadcast_to(jnp.sum(jnp.where(here, table, 0.0), axis=1, keepdims=True), scale_ref.shape)
    for j in range(0, middle, step):
        copies[j // step].wait()
        up = jnp.dot(x, up_ref[:, j:j + step], preferred_element_type=jnp.float32)
        hidden_ref[:, j:j + step] = (up / (1.0 + jnp.exp(-up))).astype(jnp.bfloat16)


def first_up(mine, own, other, w_up):
    rows = own.shape[0]
    width, middle = w_up.shape
    vmem, hbm = pl.BlockSpec(memory_space=pltpu.VMEM), pl.BlockSpec(memory_space=pltpu.HBM)
    return pl.pallas_call(
        first_up_body,
        out_shape=[
            pltpu.VMEM((2 * rows, middle), jnp.bfloat16),
            pltpu.VMEM((2 * rows, LANES), jnp.float32),
            pltpu.VMEM(w_up.shape, w_up.dtype),
        ],
        in_specs=[pl.BlockSpec(memory_space=pltpu.SMEM), vmem, vmem, hbm],
        out_specs=[vmem] * 3,
        scratch_shapes=[pltpu.SemaphoreType.DMA((middle // step_of(middle, 256),))],
        compiler_params=pltpu.CompilerParams(vmem_limit_bytes=16 * 2**20),
        cost_estimate=pl.CostEstimate(
            flops=4 * rows * width * middle, bytes_accessed=2 * width * middle, transcendentals=2 * rows * middle
        ),
    )(mine, own, other, pltpu.with_memory_space_constraint(w_up, pltpu.HBM))


def first_down_body(hidden_ref, scale_ref, down_hbm, out_own, out_other, down_ref, sems):
    middle, width = down_ref.shape
    step = step_of(width, 512)
    copies = []
    for j in range(0, width, step):
        s = pl.ds(j, step)
        copies.append(pltpu.make_async_copy(down_hbm.at[:, s], down_ref.at[:, s], sems.at[len(copies)]))
        copies[-1].start()
    rows = out_own.shape[0]
    scale = scale_ref[:, :1]
    hidden = hidden_ref[...]
    for j in range(0, width, step):
        copies[j // step].wait()
        answer = jnp.dot(hidden, down_ref[:, j:j + step], preferred_element_type=jnp.float32)
        answer = answer.astype(jnp.bfloat16).astype(jnp.float32) * scale
        out_own[:, j:j + step] = answer[:rows]
        out_other[:, j:j + step] = answer[rows:]


def first_down(hidden, scale, w_down):
    rows = hidden.shape[0] // 2
    middle, width = w_down.shape
    vmem, hbm = pl.BlockSpec(memory_space=pltpu.VMEM), pl.BlockSpec(memory_space=pltpu.HBM)
    return pl.pallas_call(
        first_down_body,
        out_shape=[pltpu.VMEM((rows, width), jnp.float32)] * 2 + [pltpu.VMEM(w_down.shape, w_down.dtype)],
        in_specs=[vmem, vmem, hbm],
        out_specs=[vmem] * 3,
        scratch_shapes=[pltpu.SemaphoreType.DMA((width // step_of(width, 512),))],
        compiler_params=pltpu.CompilerParams(vmem_limit_bytes=16 * 2**20),
        cost_estimate=pl.CostEstimate(
            flops=4 * rows * width * middle, bytes_accessed=2 * width * middle, transcendentals=0
        ),
    )(hidden, scale, pltpu.with_memory_space_constraint(w_down, pltpu.HBM))


def label_body(tokens_ref, ids_ref, weights_ref, out_ref):
    rows, width = tokens_ref.shape
    columns = out_ref.shape[1] - width
    expert_of = lax.broadcasted_iota(jnp.int32, (columns, rows), 0)
    weights = weights_ref[...].astype(jnp.float32)
    table = jnp.zeros((columns, rows), jnp.float32)
    for k in range(ids_ref.shape[0]):
        table = jnp.where(ids_ref[k:k + 1, :] == expert_of, weights[k:k + 1, :], table)
    one = lax.broadcasted_iota(jnp.int32, (rows, rows), 0) == lax.broadcasted_iota(jnp.int32, (rows, rows), 1)
    turned = lax.dot_general(
        one.astype(jnp.bfloat16),
        table.astype(jnp.bfloat16),
        (((1,), (1,)), ((), ())),
        preferred_element_type=jnp.float32,
    )
    out_ref[:, :width] = tokens_ref[...]
    out_ref[:, width:] = turned.astype(jnp.bfloat16)


def label(tokens, expert_ids, route_weights, columns):
    rows, width = tokens.shape
    vmem = pl.BlockSpec(memory_space=pltpu.VMEM)
    return pl.pallas_call(
        label_body,
        out_shape=pltpu.VMEM((rows, width + columns), jnp.bfloat16),
        in_specs=[vmem] * 3,
        out_specs=vmem,
    )(tokens, expert_ids.T, route_weights.T)


def ring_plan(tokens, expert_ids, route_weights, w_up, w_down):
    rows, width = tokens.shape
    experts = lax.axis_size(BOTH)
    n = lax.axis_size("local")
    half = n // 2
    mine = lax.axis_index(BOTH).astype(jnp.int32)[None]
    order = list(range(0, n, 2)) + list(range(n - 1, 0, -2))
    onward = [(order[i], order[(i + 1) % n]) for i in range(n)]
    pairs = onward + [(n + b, n + a) for a, b in onward]
    def hop(x):
        return lax.ppermute(x, BOTH, pairs)

    def swap(x):
        return lax.ppermute(x, "node", [(0, 1), (1, 0)])

    def bf(x):
        return x.astype(jnp.bfloat16)

    columns = -(-experts // LANES) * LANES
    own = label(tokens, expert_ids, route_weights, columns)

    a, b = [own], [swap(own)]
    ahead_a, ahead_b = [None], [None]
    behind, ahead = {}, {}

    def compute(h, first=None):
        blocks = (a[h], b[h], ahead_a[h], ahead_b[h])
        if first is not None:
            blocks, _ = lax.optimization_barrier((blocks, first))
        r = expert(mine, blocks, (False, False, True, True), up, down)
        behind[h], ahead[h] = r[:2], r[2:]

    hidden, scale, up = first_up(mine, own, b[0], w_up[0])
    for h in range(1, half + 1):
        a.append(hop(a[-1]))
        if h < half:
            b.append(hop(b[-1]))
        if h == 1:
            a[1], hidden, up = lax.optimization_barrier((a[1], hidden, up))
            up = pltpu.with_memory_space_constraint(up, pltpu.VMEM)
        elif h == 2:
            own_a, own_b, down = first_down(hidden, scale, w_down[0])
            a[2], own_a, own_b, down = lax.optimization_barrier((a[2], own_a, own_b, down))
            down = pltpu.with_memory_space_constraint(down, pltpu.VMEM)
        elif h < half:
            compute(h - 2)
            a[h], behind[h - 2], ahead[h - 2] = lax.optimization_barrier((a[h], behind[h - 2], ahead[h - 2]))
        if 1 < h < half:
            a[h], ahead_a[h - 1], ahead_b[h - 1] = lax.optimization_barrier((a[h], ahead_a[h - 1], ahead_b[h - 1]))
        if h < half:
            ahead_b.append(swap(a[h]))
            ahead_a.append(swap(b[h]))
    compute(half - 2, b[half - 1])
    compute(half - 1, behind[half - 2])
    a[half], behind[half - 1], ahead[half - 1] = lax.optimization_barrier((a[half], behind[half - 1], ahead[half - 1]))
    ahead_b.append(swap(a[half]))

    def join(x, y):
        return x.astype(jnp.float32) + y.astype(jnp.float32)

    def total(h, after=None):
        mine_a, mine_b = behind[h]
        if after is not None:
            mine_a, mine_b, _ = lax.optimization_barrier((mine_a, mine_b, after))
        sum_b = join(ahead[h][1], swap(mine_a))
        return [join(ahead[h][0], swap(mine_b)), sum_b]

    sums = {half - 1: total(half - 1)}
    send_b = bf(sums[half - 1][1])
    run_b = hop(send_b)
    last_blocks, send_b, sums[half - 1] = lax.optimization_barrier(((a[half], ahead_b[half]), send_b, sums[half - 1]))
    far = expert(mine, last_blocks, (True, False), up, down)
    sums[half - 2] = total(half - 2, far[0])
    run_a = hop(bf(join(far[0], swap(far[1]))))
    for h in range(half - 1, 0, -1):
        if h < half - 1:
            run_b = hop(bf(join(sums[h][1], run_b)))
        if h - 1 > 0 and h - 1 not in sums:
            sums[h - 1] = total(h - 1, run_a)
        run_a = hop(bf(join(sums[h][0], run_a)))
    last = swap(bf(join(own_b, run_b)))
    return bf(join(join(own_a, run_a), last))


def solution(mesh):
    placed = (
        P(("rep", "node", "local"), None),
        P(("rep", "node", "local"), None),
        P(("rep", "node", "local"), None),
        P(("node", "local"), None, None),
        P(("node", "local"), None, None),
    )
    n = mesh.shape["local"]
    ringed = mesh.shape["node"] == 2 and n % 2 == 0 and 6 <= n <= 16
    return jax.shard_map(
        ring_plan if ringed else gather_plan,
        mesh=mesh,
        in_specs=placed,
        out_specs=P(("rep", "node", "local"), None),
        check_vma=False,
    )
```

```python
import functools
import jax
import jax.numpy as jnp
from jax import lax
from jax.experimental import pallas as pl
from jax.experimental.pallas import tpu as pltpu
from jax.sharding import PartitionSpec as P

BOTH = ("node", "local")
LANES = 128
LATE = (3, 4)


def gather_plan(tokens, expert_ids, route_weights, w_up, w_down):
    mine = lax.axis_index(BOTH)
    everyone = lax.all_gather(tokens, BOTH, tiled=True)
    ids = lax.all_gather(expert_ids, BOTH, tiled=True)
    weights = lax.all_gather(route_weights, BOTH, tiled=True)
    scale = jnp.sum(jnp.where(ids == mine, weights.astype(jnp.float32), 0.0), axis=1)
    hidden = jax.nn.silu(jnp.dot(everyone, w_up[0], preferred_element_type=jnp.float32)).astype(jnp.bfloat16)
    answer = jnp.dot(hidden, w_down[0], preferred_element_type=jnp.float32)
    part = (answer * scale[:, None]).astype(jnp.bfloat16)
    return lax.psum_scatter(part, BOTH, scatter_dimension=0, tiled=True)


def step_of(size, wanted):
    step = wanted
    while step > LANES and size % step:
        step //= 2
    return step if size % step == 0 else size


def expert_body(blocks, parts, mine_ref, *refs):
    tokens = refs[:blocks]
    up_ref, downs = refs[blocks], refs[blocks + 1:blocks + 1 + parts]
    outs = refs[blocks + 1 + parts:2 * blocks + 1 + parts]
    hidden_ref = refs[2 * blocks + 1 + parts]
    width, middle = up_ref.shape
    rows = tokens[0].shape[0]
    x = jnp.concatenate([t[:, :width] for t in tokens], axis=0)
    table = jnp.concatenate([t[:, width:] for t in tokens], axis=0).astype(jnp.float32)
    here = lax.broadcasted_iota(jnp.int32, table.shape, 1) == mine_ref[0]
    scale = jnp.sum(jnp.where(here, table, 0.0), axis=1, keepdims=True)
    step = step_of(middle, 256)
    for j in range(0, middle, step):
        up = jnp.dot(x, up_ref[:, j:j + step], preferred_element_type=jnp.float32)
        hidden_ref[:, j:j + step] = (up / (1.0 + jnp.exp(-up))).astype(jnp.bfloat16)
    hidden = hidden_ref[...]
    at = 0
    for down_ref in downs:
        step = step_of(down_ref.shape[1], 512)
        for j in range(0, down_ref.shape[1], step):
            answer = jnp.dot(hidden, down_ref[:, j:j + step], preferred_element_type=jnp.float32)
            answer = answer.astype(jnp.bfloat16).astype(jnp.float32) * scale
            for i in range(blocks):
                outs[i][:, at:at + step] = answer[i * rows:(i + 1) * rows].astype(outs[i].dtype)
            at += step


def expert(mine, blocks, kept, up, down):
    rows = blocks[0].shape[0]
    width, middle = up.shape
    total = rows * len(blocks)
    vmem = pl.BlockSpec(memory_space=pltpu.VMEM)
    return pl.pallas_call(
        functools.partial(expert_body, len(blocks), len(down)),
        out_shape=[
            jax.ShapeDtypeStruct((rows, width), jnp.float32 if k else jnp.bfloat16) for k in kept
        ],
        in_specs=[pl.BlockSpec(memory_space=pltpu.SMEM)] + [vmem] * (len(blocks) + 1 + len(down)),
        out_specs=[vmem] * len(blocks),
        scratch_shapes=[pltpu.VMEM((total, middle), jnp.bfloat16)],
        compiler_params=pltpu.CompilerParams(vmem_limit_bytes=16 * 2**20),
        cost_estimate=pl.CostEstimate(
            flops=4 * total * width * middle, bytes_accessed=4 * width * middle, transcendentals=total * middle
        ),
    )(mine, *blocks, up, *down)


def load_body(first, pieces, source, out, sems):
    height, columns = out.shape[0] // pieces, out.shape[1]
    copies = []
    for i in range(pieces):
        s = pl.ds(i * height, height)
        copies.append(pltpu.make_async_copy(source.at[s, pl.ds(first, columns)], out.at[s], sems.at[i]))
        copies[-1].start()
    for c in copies:
        c.wait()


def load(matrix, first, last, after):
    matrix, _ = lax.optimization_barrier((matrix, after))
    height = matrix.shape[0]
    pieces = 8 if height % (8 * 16) == 0 else 1
    return pl.pallas_call(
        functools.partial(load_body, first, pieces),
        out_shape=pltpu.VMEM((height, last - first), matrix.dtype),
        in_specs=[pl.BlockSpec(memory_space=pltpu.HBM)],
        out_specs=pl.BlockSpec(memory_space=pltpu.VMEM),
        scratch_shapes=[pltpu.SemaphoreType.DMA((pieces,))],
        compiler_params=pltpu.CompilerParams(vmem_limit_bytes=16 * 2**20),
    )(pltpu.with_memory_space_constraint(matrix, pltpu.HBM))


def label_body(tokens_ref, ids_ref, weights_ref, out_ref):
    rows, width = tokens_ref.shape
    columns = out_ref.shape[1] - width
    expert_of = lax.broadcasted_iota(jnp.int32, (columns, rows), 0)
    weights = weights_ref[...].astype(jnp.float32)
    table = jnp.zeros((columns, rows), jnp.float32)
    for k in range(ids_ref.shape[0]):
        table = jnp.where(ids_ref[k:k + 1, :] == expert_of, weights[k:k + 1, :], table)
    one = lax.broadcasted_iota(jnp.int32, (rows, rows), 0) == lax.broadcasted_iota(jnp.int32, (rows, rows), 1)
    turned = lax.dot_general(
        one.astype(jnp.bfloat16),
        table.astype(jnp.bfloat16),
        (((1,), (1,)), ((), ())),
        preferred_element_type=jnp.float32,
    )
    out_ref[:, :width] = tokens_ref[...]
    out_ref[:, width:] = turned.astype(jnp.bfloat16)


def label(tokens, expert_ids, route_weights, columns):
    rows, width = tokens.shape
    vmem = pl.BlockSpec(memory_space=pltpu.VMEM)
    return pl.pallas_call(
        label_body,
        out_shape=pltpu.VMEM((rows, width + columns), jnp.bfloat16),
        in_specs=[vmem] * 3,
        out_specs=vmem,
    )(tokens, expert_ids.T, route_weights.T)


def ring_plan(tokens, expert_ids, route_weights, w_up, w_down):
    rows, width = tokens.shape
    experts = lax.axis_size(BOTH)
    n = lax.axis_size("local")
    half = n // 2
    mine = lax.axis_index(BOTH).astype(jnp.int32)[None]
    order = list(range(0, n, 2)) + list(range(n - 1, 0, -2))
    onward = [(order[i], order[(i + 1) % n]) for i in range(n)]
    pairs = onward + [(n + b, n + a) for a, b in onward]
    def hop(x):
        return lax.ppermute(x, BOTH, pairs)

    def swap(x):
        return lax.ppermute(x, "node", [(0, 1), (1, 0)])

    def bf(x):
        return x.astype(jnp.bfloat16)

    columns = -(-experts // LANES) * LANES
    own = label(tokens, expert_ids, route_weights, columns)

    a, b = [own], [swap(own)]
    ahead_a, ahead_b = [None], [None]
    behind, ahead = {}, {}

    def compute(h, first=None):
        blocks = (a[h], b[h], ahead_a[h], ahead_b[h])
        if first is not None:
            blocks, _ = lax.optimization_barrier((blocks, first))
        r = expert(mine, blocks, (False, False, True, True), up, down)
        behind[h], ahead[h] = r[:2], r[2:]

    step = step_of(width, 512)
    cut = (width // step * LATE[0] // LATE[1]) * step
    up, mine = lax.optimization_barrier((load(w_up[0], 0, w_up.shape[2], b[0]), mine))
    for h in range(1, half + 1):
        a.append(hop(a[-1]))
        if h < half:
            b.append(hop(b[-1]))
        if h == 1:
            a[1], up = lax.optimization_barrier((a[1], up))
            up = pltpu.with_memory_space_constraint(up, pltpu.VMEM)
        elif h == 2:
            down = load(w_down[0], 0, cut, a[1])
            a[2], down_first = lax.optimization_barrier((a[2], down))
        elif h == 3:
            down = load(w_down[0], cut, width, a[2])
            a[3], down_last = lax.optimization_barrier((a[3], down))
        if 1 < h < half:
            a[h], ahead_a[h - 1], ahead_b[h - 1] = lax.optimization_barrier((a[h], ahead_a[h - 1], ahead_b[h - 1]))
        if h < half:
            ahead_b.append(swap(a[h]))
            ahead_a.append(swap(b[h]))
    down = [pltpu.with_memory_space_constraint(d, pltpu.VMEM) for d in (down_first, down_last)]
    near = range(1, half - 2)
    blocks = [a[0], b[0]]
    for h in near:
        blocks += [a[h], b[h], ahead_a[h], ahead_b[h]]
    blocks, _ = lax.optimization_barrier((blocks, a[half - 1]))
    r = expert(mine, blocks, (True, True) + (False, False, True, True) * len(near), up, down)
    r, a[half] = lax.optimization_barrier((r, a[half]))
    own_a, own_b = r[:2]
    for i, h in enumerate(near):
        behind[h], ahead[h] = r[4 * i + 2:4 * i + 4], r[4 * i + 4:4 * i + 6]
    ahead_b.append(swap(a[half]))
    h = half - 1
    r = expert(
        mine,
        (a[h], b[h], ahead_a[h], ahead_b[h], a[half], ahead_b[half]),
        (False, False, True, True, True, False),
        up,
        down,
    )
    behind[h], ahead[h], far = r[:2], r[2:4], r[4:]

    def join(x, y):
        return x.astype(jnp.float32) + y.astype(jnp.float32)

    def total(h, after=None):
        mine_a, mine_b = behind[h]
        if after is not None:
            mine_a, mine_b, _ = lax.optimization_barrier((mine_a, mine_b, after))
        sum_b = join(ahead[h][1], swap(mine_a))
        return [join(ahead[h][0], swap(mine_b)), sum_b]

    send_a = bf(join(far[0], swap(far[1])))
    sums = {half - 1: total(half - 1)}
    send_b = bf(sums[half - 1][1])
    run_a = hop(send_a)
    run_b = hop(send_b)
    compute(half - 2, (send_a, send_b))
    sums[half - 2] = total(half - 2)
    for h in range(half - 1, 0, -1):
        if h < half - 1:
            run_b = hop(bf(join(sums[h][1], run_b)))
        if h - 1 > 0 and h - 1 not in sums:
            sums[h - 1] = total(h - 1, run_a)
        send_a = bf(join(sums[h][0], run_a))
        run_a = hop(send_a)
    last = swap(bf(join(own_b, run_b)))
    return bf(join(join(own_a, run_a), last))


def solution(mesh):
    placed = (
        P(("rep", "node", "local"), None),
        P(("rep", "node", "local"), None),
        P(("rep", "node", "local"), None),
        P(("node", "local"), None, None),
        P(("node", "local"), None, None),
    )
    n = mesh.shape["local"]
    ringed = mesh.shape["node"] == 2 and n % 2 == 0 and 6 <= n <= 16
    return jax.shard_map(
        ring_plan if ringed else gather_plan,
        mesh=mesh,
        in_specs=placed,
        out_specs=P(("rep", "node", "local"), None),
        check_vma=False,
    )
```

```python
import functools
import jax
import jax.numpy as jnp
from jax import lax
from jax.experimental import pallas as pl
from jax.experimental.pallas import tpu as pltpu
from jax.sharding import PartitionSpec as P

BOTH = ("node", "local")
LANES = 128
LATE = (3, 4)


def gather_plan(tokens, expert_ids, route_weights, w_up, w_down):
    mine = lax.axis_index(BOTH)
    everyone = lax.all_gather(tokens, BOTH, tiled=True)
    ids = lax.all_gather(expert_ids, BOTH, tiled=True)
    weights = lax.all_gather(route_weights, BOTH, tiled=True)
    scale = jnp.sum(jnp.where(ids == mine, weights.astype(jnp.float32), 0.0), axis=1)
    hidden = jax.nn.silu(jnp.dot(everyone, w_up[0], preferred_element_type=jnp.float32)).astype(jnp.bfloat16)
    answer = jnp.dot(hidden, w_down[0], preferred_element_type=jnp.float32)
    part = (answer * scale[:, None]).astype(jnp.bfloat16)
    return lax.psum_scatter(part, BOTH, scatter_dimension=0, tiled=True)


def step_of(size, wanted):
    step = wanted
    while step > LANES and size % step:
        step //= 2
    return step if size % step == 0 else size


def expert_body(blocks, parts, mine_ref, *refs):
    tokens = refs[:blocks]
    up_ref, downs = refs[blocks], refs[blocks + 1:blocks + 1 + parts]
    outs = refs[blocks + 1 + parts:2 * blocks + 1 + parts]
    hidden_ref = refs[2 * blocks + 1 + parts]
    width, middle = up_ref.shape
    rows = tokens[0].shape[0]
    x = jnp.concatenate([t[:, :width] for t in tokens], axis=0)
    table = jnp.concatenate([t[:, width:] for t in tokens], axis=0).astype(jnp.float32)
    here = lax.broadcasted_iota(jnp.int32, table.shape, 1) == mine_ref[0]
    scale = jnp.sum(jnp.where(here, table, 0.0), axis=1, keepdims=True)
    step = step_of(middle, 256)
    for j in range(0, middle, step):
        up = jnp.dot(x, up_ref[:, j:j + step], preferred_element_type=jnp.float32)
        hidden_ref[:, j:j + step] = (up / (1.0 + jnp.exp(-up))).astype(jnp.bfloat16)
    hidden = hidden_ref[...]
    at = 0
    for down_ref in downs:
        step = step_of(down_ref.shape[1], 512)
        for j in range(0, down_ref.shape[1], step):
            answer = jnp.dot(hidden, down_ref[:, j:j + step], preferred_element_type=jnp.float32)
            answer = answer.astype(jnp.bfloat16).astype(jnp.float32) * scale
            for i in range(blocks):
                outs[i][:, at:at + step] = answer[i * rows:(i + 1) * rows].astype(outs[i].dtype)
            at += step


def expert(mine, blocks, kept, up, down):
    rows = blocks[0].shape[0]
    width, middle = up.shape
    total = rows * len(blocks)
    vmem = pl.BlockSpec(memory_space=pltpu.VMEM)
    return pl.pallas_call(
        functools.partial(expert_body, len(blocks), len(down)),
        out_shape=[
            jax.ShapeDtypeStruct((rows, width), jnp.float32 if k else jnp.bfloat16) for k in kept
        ],
        in_specs=[pl.BlockSpec(memory_space=pltpu.SMEM)] + [vmem] * (len(blocks) + 1 + len(down)),
        out_specs=[vmem] * len(blocks),
        scratch_shapes=[pltpu.VMEM((total, middle), jnp.bfloat16)],
        compiler_params=pltpu.CompilerParams(vmem_limit_bytes=16 * 2**20),
        cost_estimate=pl.CostEstimate(
            flops=4 * total * width * middle, bytes_accessed=4 * width * middle, transcendentals=total * middle
        ),
    )(mine, *blocks, up, *down)


def load_body(first, pieces, source, out, sems):
    height, columns = out.shape[0] // pieces, out.shape[1]
    copies = []
    for i in range(pieces):
        s = pl.ds(i * height, height)
        copies.append(pltpu.make_async_copy(source.at[s, pl.ds(first, columns)], out.at[s], sems.at[i]))
        copies[-1].start()
    for c in copies:
        c.wait()


def load(matrix, first, last, after):
    matrix, _ = lax.optimization_barrier((matrix, after))
    height = matrix.shape[0]
    pieces = 8 if height % (8 * 16) == 0 else 1
    return pl.pallas_call(
        functools.partial(load_body, first, pieces),
        out_shape=pltpu.VMEM((height, last - first), matrix.dtype),
        in_specs=[pl.BlockSpec(memory_space=pltpu.HBM)],
        out_specs=pl.BlockSpec(memory_space=pltpu.VMEM),
        scratch_shapes=[pltpu.SemaphoreType.DMA((pieces,))],
        compiler_params=pltpu.CompilerParams(vmem_limit_bytes=16 * 2**20),
    )(pltpu.with_memory_space_constraint(matrix, pltpu.HBM))


def label_body(tokens_ref, ids_ref, weights_ref, out_ref):
    rows, width = tokens_ref.shape
    columns = out_ref.shape[1] - width
    expert_of = lax.broadcasted_iota(jnp.int32, (columns, rows), 0)
    weights = weights_ref[...].astype(jnp.float32)
    table = jnp.zeros((columns, rows), jnp.float32)
    for k in range(ids_ref.shape[0]):
        table = jnp.where(ids_ref[k:k + 1, :] == expert_of, weights[k:k + 1, :], table)
    one = lax.broadcasted_iota(jnp.int32, (rows, rows), 0) == lax.broadcasted_iota(jnp.int32, (rows, rows), 1)
    turned = lax.dot_general(
        one.astype(jnp.bfloat16),
        table.astype(jnp.bfloat16),
        (((1,), (1,)), ((), ())),
        preferred_element_type=jnp.float32,
    )
    out_ref[:, :width] = tokens_ref[...]
    out_ref[:, width:] = turned.astype(jnp.bfloat16)


def label(tokens, expert_ids, route_weights, columns):
    rows, width = tokens.shape
    vmem = pl.BlockSpec(memory_space=pltpu.VMEM)
    return pl.pallas_call(
        label_body,
        out_shape=pltpu.VMEM((rows, width + columns), jnp.bfloat16),
        in_specs=[vmem] * 3,
        out_specs=vmem,
    )(tokens, expert_ids.T, route_weights.T)


def ring_plan(tokens, expert_ids, route_weights, w_up, w_down):
    rows, width = tokens.shape
    experts = lax.axis_size(BOTH)
    n = lax.axis_size("local")
    half = n // 2
    mine = lax.axis_index(BOTH).astype(jnp.int32)[None]
    order = list(range(0, n, 2)) + list(range(n - 1, 0, -2))
    onward = [(order[i], order[(i + 1) % n]) for i in range(n)]
    pairs = onward + [(n + b, n + a) for a, b in onward]
    def hop(x):
        return lax.ppermute(x, BOTH, pairs)

    def swap(x):
        return lax.ppermute(x, "node", [(0, 1), (1, 0)])

    def bf(x):
        return x.astype(jnp.bfloat16)

    columns = -(-experts // LANES) * LANES
    own = label(tokens, expert_ids, route_weights, columns)

    a, b = [own], [swap(own)]
    ahead_a, ahead_b = [None], [None]
    behind, ahead = {}, {}

    def compute(h, first=None):
        blocks = (a[h], b[h], ahead_a[h], ahead_b[h])
        if first is not None:
            blocks, _ = lax.optimization_barrier((blocks, first))
        r = expert(mine, blocks, (False, False, True, True), up, down)
        behind[h], ahead[h] = r[:2], r[2:]

    step = step_of(width, 512)
    cut = (width // step * LATE[0] // LATE[1]) * step
    up, mine = lax.optimization_barrier((load(w_up[0], 0, w_up.shape[2], b[0]), mine))
    for h in range(1, half + 1):
        a.append(hop(a[-1]))
        if h < half:
            b.append(hop(b[-1]))
        if h == 1:
            a[1], up = lax.optimization_barrier((a[1], up))
            up = pltpu.with_memory_space_constraint(up, pltpu.VMEM)
        elif h == 2:
            down = load(w_down[0], 0, cut, a[1])
            a[2], down_first = lax.optimization_barrier((a[2], down))
        elif h == 3:
            down = load(w_down[0], cut, width, a[2])
            a[3], down_last = lax.optimization_barrier((a[3], down))
        if 1 < h < half:
            a[h], ahead_a[h - 1], ahead_b[h - 1] = lax.optimization_barrier((a[h], ahead_a[h - 1], ahead_b[h - 1]))
        if h < half:
            ahead_b.append(swap(a[h]))
            ahead_a.append(swap(b[h]))
    down = [pltpu.with_memory_space_constraint(d, pltpu.VMEM) for d in (down_first, down_last)]
    near = range(1, half - 2)
    blocks = [a[0], b[0]]
    for h in near:
        blocks += [a[h], b[h], ahead_a[h], ahead_b[h]]
    blocks, _ = lax.optimization_barrier((blocks, a[half - 1]))
    r = expert(mine, blocks, (True, True) + (False, False, True, True) * len(near), up, down)
    r, a[half] = lax.optimization_barrier((r, a[half]))
    own_a, own_b = r[:2]
    for i, h in enumerate(near):
        behind[h], ahead[h] = r[4 * i + 2:4 * i + 4], r[4 * i + 4:4 * i + 6]
    ahead_b.append(swap(a[half]))
    h = half - 1
    r = expert(
        mine,
        (a[h], b[h], ahead_a[h], ahead_b[h], a[half], ahead_b[half]),
        (False, False, True, True, True, False),
        up,
        down,
    )
    behind[h], ahead[h], far = r[:2], r[2:4], r[4:]

    def join(x, y):
        return x.astype(jnp.float32) + y.astype(jnp.float32)

    def total(h, after=None):
        mine_a, mine_b = behind[h]
        if after is not None:
            mine_a, mine_b, _ = lax.optimization_barrier((mine_a, mine_b, after))
        sum_b = join(ahead[h][1], swap(mine_a))
        return [join(ahead[h][0], swap(mine_b)), sum_b]

    send_a = bf(join(far[0], swap(far[1])))
    sums = {half - 1: total(half - 1)}
    send_b = bf(sums[half - 1][1])
    run_a = hop(send_a)
    run_b = hop(send_b)
    compute(half - 2, (send_a, send_b))
    sums[half - 2] = total(half - 2)
    for h in range(half - 1, 0, -1):
        if h < half - 1:
            run_b = hop(bf(join(sums[h][1], run_b)))
        send_a = bf(join(sums[h][0], run_a))
        if h - 1 > 0 and h - 1 not in sums:
            sums[h - 1] = total(h - 1, send_a)
        run_a = hop(send_a)
    last = swap(bf(join(own_b, run_b)))
    return bf(join(join(own_a, run_a), last))


def solution(mesh):
    placed = (
        P(("rep", "node", "local"), None),
        P(("rep", "node", "local"), None),
        P(("rep", "node", "local"), None),
        P(("node", "local"), None, None),
        P(("node", "local"), None, None),
    )
    n = mesh.shape["local"]
    ringed = mesh.shape["node"] == 2 and n % 2 == 0 and 6 <= n <= 16
    return jax.shard_map(
        ring_plan if ringed else gather_plan,
        mesh=mesh,
        in_specs=placed,
        out_specs=P(("rep", "node", "local"), None),
        check_vma=False,
    )
```

```python
import functools
import jax
import jax.numpy as jnp
from jax import lax
from jax.experimental import pallas as pl
from jax.experimental.pallas import tpu as pltpu
from jax.sharding import PartitionSpec as P

BOTH = ("node", "local")
LANES = 128
LATE = (3, 4)


def gather_plan(tokens, expert_ids, route_weights, w_up, w_down):
    mine = lax.axis_index(BOTH)
    everyone = lax.all_gather(tokens, BOTH, tiled=True)
    ids = lax.all_gather(expert_ids, BOTH, tiled=True)
    weights = lax.all_gather(route_weights, BOTH, tiled=True)
    scale = jnp.sum(jnp.where(ids == mine, weights.astype(jnp.float32), 0.0), axis=1)
    hidden = jax.nn.silu(jnp.dot(everyone, w_up[0], preferred_element_type=jnp.float32)).astype(jnp.bfloat16)
    answer = jnp.dot(hidden, w_down[0], preferred_element_type=jnp.float32)
    part = (answer * scale[:, None]).astype(jnp.bfloat16)
    return lax.psum_scatter(part, BOTH, scatter_dimension=0, tiled=True)


def step_of(size, wanted):
    step = wanted
    while step > LANES and size % step:
        step //= 2
    return step if size % step == 0 else size


def expert_body(blocks, parts, mine_ref, *refs):
    tokens = refs[:blocks]
    up_ref, downs = refs[blocks], refs[blocks + 1:blocks + 1 + parts]
    outs = refs[blocks + 1 + parts:2 * blocks + 1 + parts]
    hidden_ref = refs[2 * blocks + 1 + parts]
    width, middle = up_ref.shape
    rows = tokens[0].shape[0]
    x = jnp.concatenate([t[:, :width] for t in tokens], axis=0)
    table = jnp.concatenate([t[:, width:] for t in tokens], axis=0).astype(jnp.float32)
    here = lax.broadcasted_iota(jnp.int32, table.shape, 1) == mine_ref[0]
    scale = jnp.sum(jnp.where(here, table, 0.0), axis=1, keepdims=True)
    step = step_of(middle, 256)
    for j in range(0, middle, step):
        up = jnp.dot(x, up_ref[:, j:j + step], preferred_element_type=jnp.float32)
        hidden_ref[:, j:j + step] = (up / (1.0 + jnp.exp(-up))).astype(jnp.bfloat16)
    hidden = hidden_ref[...]
    at = 0
    for down_ref in downs:
        step = step_of(down_ref.shape[1], 512)
        for j in range(0, down_ref.shape[1], step):
            answer = jnp.dot(hidden, down_ref[:, j:j + step], preferred_element_type=jnp.float32)
            answer = answer.astype(jnp.bfloat16).astype(jnp.float32) * scale
            for i in range(blocks):
                outs[i][:, at:at + step] = answer[i * rows:(i + 1) * rows].astype(outs[i].dtype)
            at += step


def expert(mine, blocks, kept, up, down):
    rows = blocks[0].shape[0]
    width, middle = up.shape
    total = rows * len(blocks)
    vmem = pl.BlockSpec(memory_space=pltpu.VMEM)
    return pl.pallas_call(
        functools.partial(expert_body, len(blocks), len(down)),
        out_shape=[
            jax.ShapeDtypeStruct((rows, width), jnp.float32 if k else jnp.bfloat16) for k in kept
        ],
        in_specs=[pl.BlockSpec(memory_space=pltpu.SMEM)] + [vmem] * (len(blocks) + 1 + len(down)),
        out_specs=[vmem] * len(blocks),
        scratch_shapes=[pltpu.VMEM((total, middle), jnp.bfloat16)],
        compiler_params=pltpu.CompilerParams(vmem_limit_bytes=16 * 2**20),
        cost_estimate=pl.CostEstimate(
            flops=4 * total * width * middle, bytes_accessed=4 * width * middle, transcendentals=total * middle
        ),
    )(mine, *blocks, up, *down)


def load_body(first, pieces, source, out, sems):
    height, columns = out.shape[0] // pieces, out.shape[1]
    copies = []
    for i in range(pieces):
        s = pl.ds(i * height, height)
        copies.append(pltpu.make_async_copy(source.at[s, pl.ds(first, columns)], out.at[s], sems.at[i]))
        copies[-1].start()
    for c in copies:
        c.wait()


def load(matrix, first, last, after):
    matrix, _ = lax.optimization_barrier((matrix, after))
    height = matrix.shape[0]
    pieces = 8 if height % (8 * 16) == 0 else 1
    return pl.pallas_call(
        functools.partial(load_body, first, pieces),
        out_shape=pltpu.VMEM((height, last - first), matrix.dtype),
        in_specs=[pl.BlockSpec(memory_space=pltpu.HBM)],
        out_specs=pl.BlockSpec(memory_space=pltpu.VMEM),
        scratch_shapes=[pltpu.SemaphoreType.DMA((pieces,))],
        compiler_params=pltpu.CompilerParams(vmem_limit_bytes=16 * 2**20),
    )(pltpu.with_memory_space_constraint(matrix, pltpu.HBM))


def label_body(tokens_ref, ids_ref, weights_ref, out_ref):
    rows, width = tokens_ref.shape
    columns = out_ref.shape[1] - width
    expert_of = lax.broadcasted_iota(jnp.int32, (columns, rows), 0)
    weights = weights_ref[...].astype(jnp.float32)
    table = jnp.zeros((columns, rows), jnp.float32)
    for k in range(ids_ref.shape[0]):
        table = jnp.where(ids_ref[k:k + 1, :] == expert_of, weights[k:k + 1, :], table)
    one = lax.broadcasted_iota(jnp.int32, (rows, rows), 0) == lax.broadcasted_iota(jnp.int32, (rows, rows), 1)
    turned = lax.dot_general(
        one.astype(jnp.bfloat16),
        table.astype(jnp.bfloat16),
        (((1,), (1,)), ((), ())),
        preferred_element_type=jnp.float32,
    )
    out_ref[:, :width] = tokens_ref[...]
    out_ref[:, width:] = turned.astype(jnp.bfloat16)


def label(tokens, expert_ids, route_weights, columns):
    rows, width = tokens.shape
    vmem = pl.BlockSpec(memory_space=pltpu.VMEM)
    return pl.pallas_call(
        label_body,
        out_shape=pltpu.VMEM((rows, width + columns), jnp.bfloat16),
        in_specs=[vmem] * 3,
        out_specs=vmem,
    )(tokens, expert_ids.T, route_weights.T)


def ring_plan(tokens, expert_ids, route_weights, w_up, w_down):
    rows, width = tokens.shape
    experts = lax.axis_size(BOTH)
    n = lax.axis_size("local")
    half = n // 2
    mine = lax.axis_index(BOTH).astype(jnp.int32)[None]
    order = list(range(0, n, 2)) + list(range(n - 1, 0, -2))
    onward = [(order[i], order[(i + 1) % n]) for i in range(n)]
    pairs = onward + [(n + b, n + a) for a, b in onward]
    def hop(x):
        return lax.ppermute(x, BOTH, pairs)

    def swap(x):
        return lax.ppermute(x, "node", [(0, 1), (1, 0)])

    def bf(x):
        return x.astype(jnp.bfloat16)

    columns = -(-experts // LANES) * LANES
    own = label(tokens, expert_ids, route_weights, columns)

    a, b = [own], [swap(own)]
    ahead_a, ahead_b = [None], [None]
    behind, ahead = {}, {}

    def compute(h, first=None):
        blocks = (a[h], b[h], ahead_a[h], ahead_b[h])
        if first is not None:
            blocks, _ = lax.optimization_barrier((blocks, first))
        r = expert(mine, blocks, (False, False, True, True), up, down)
        behind[h], ahead[h] = r[:2], r[2:]

    step = step_of(width, 512)
    cut = (width // step * LATE[0] // LATE[1]) * step
    up, mine = lax.optimization_barrier((load(w_up[0], 0, w_up.shape[2], b[0]), mine))
    for h in range(1, half + 1):
        a.append(hop(a[-1]))
        if h < half:
            b.append(hop(b[-1]))
        if h == 1:
            a[1], up = lax.optimization_barrier((a[1], up))
            up = pltpu.with_memory_space_constraint(up, pltpu.VMEM)
        elif h == 2:
            down = load(w_down[0], 0, cut, a[1])
            a[2], down_first = lax.optimization_barrier((a[2], down))
        elif h == 3:
            down = load(w_down[0], cut, width, (a[2], ahead_b[2]))
            a[3], down_last = lax.optimization_barrier((a[3], down))
        if 1 < h < half:
            a[h], ahead_a[h - 1], ahead_b[h - 1] = lax.optimization_barrier((a[h], ahead_a[h - 1], ahead_b[h - 1]))
        if h < half:
            ahead_b.append(swap(a[h]))
            ahead_a.append(swap(b[h]))
    down = [pltpu.with_memory_space_constraint(d, pltpu.VMEM) for d in (down_first, down_last)]
    near, h = range(1, half - 2), half - 1
    blocks = [a[h], ahead_b[h]]
    for i in near:
        blocks += [a[i], b[i], ahead_a[i], ahead_b[i]]
    r = expert(mine, blocks, (False, True) + (False, False, True, True) * len(near), up, down)
    r, a[half] = lax.optimization_barrier((r, a[half]))
    for i in near:
        behind[i], ahead[i] = r[4 * i - 2:4 * i], r[4 * i:4 * i + 2]
    ahead_b.append(swap(a[half]))
    last = expert(mine, (b[h], ahead_a[h], a[half], ahead_b[half]), (False, True, True, False), up, down)
    behind[h], ahead[h], far = (r[0], last[0]), (last[1], r[1]), last[2:]

    def join(x, y):
        return x.astype(jnp.float32) + y.astype(jnp.float32)

    def total(h, after=None):
        mine_a, mine_b = behind[h]
        if after is not None:
            mine_a, mine_b, _ = lax.optimization_barrier((mine_a, mine_b, after))
        sum_b = join(ahead[h][1], swap(mine_a))
        return [join(ahead[h][0], swap(mine_b)), sum_b]

    send_a = bf(join(far[0], swap(far[1])))
    sums = {half - 1: total(half - 1)}
    send_b = bf(sums[half - 1][1])
    run_a = hop(send_a)
    run_b = hop(send_b)
    compute(half - 2, (send_a, send_b))
    sums[half - 2] = total(half - 2)
    for h in range(half - 1, 0, -1):
        if h < half - 1:
            run_b = hop(bf(join(sums[h][1], run_b)))
        send_a = bf(join(sums[h][0], run_a))
        if h - 1 > 0 and h - 1 not in sums:
            sums[h - 1] = total(h - 1, send_a)
        run_a = hop(send_a)
    blocks, _ = lax.optimization_barrier(((a[0], b[0]), send_a))
    own_a, own_b = expert(mine, blocks, (True, True), up, down)
    last = swap(bf(join(own_b, run_b)))
    return bf(join(join(own_a, run_a), last))


def solution(mesh):
    placed = (
        P(("rep", "node", "local"), None),
        P(("rep", "node", "local"), None),
        P(("rep", "node", "local"), None),
        P(("node", "local"), None, None),
        P(("node", "local"), None, None),
    )
    n = mesh.shape["local"]
    ringed = mesh.shape["node"] == 2 and n % 2 == 0 and 6 <= n <= 16
    return jax.shard_map(
        ring_plan if ringed else gather_plan,
        mesh=mesh,
        in_specs=placed,
        out_specs=P(("rep", "node", "local"), None),
        check_vma=False,
    )
```

```python
import functools
import jax
import jax.numpy as jnp
from jax import lax
from jax.experimental import pallas as pl
from jax.experimental.pallas import tpu as pltpu
from jax.sharding import PartitionSpec as P

BOTH = ("node", "local")
LANES = 128
LATE = (2, 3)


def gather_plan(tokens, expert_ids, route_weights, w_up, w_down):
    mine = lax.axis_index(BOTH)
    everyone = lax.all_gather(tokens, BOTH, tiled=True)
    ids = lax.all_gather(expert_ids, BOTH, tiled=True)
    weights = lax.all_gather(route_weights, BOTH, tiled=True)
    scale = jnp.sum(jnp.where(ids == mine, weights.astype(jnp.float32), 0.0), axis=1)
    hidden = jax.nn.silu(jnp.dot(everyone, w_up[0], preferred_element_type=jnp.float32)).astype(jnp.bfloat16)
    answer = jnp.dot(hidden, w_down[0], preferred_element_type=jnp.float32)
    part = (answer * scale[:, None]).astype(jnp.bfloat16)
    return lax.psum_scatter(part, BOTH, scatter_dimension=0, tiled=True)


def step_of(size, wanted):
    step = wanted
    while step > LANES and size % step:
        step //= 2
    return step if size % step == 0 else size


def expert_body(blocks, parts, mine_ref, *refs):
    tokens = refs[:blocks]
    up_ref, downs = refs[blocks], refs[blocks + 1:blocks + 1 + parts]
    outs = refs[blocks + 1 + parts:2 * blocks + 1 + parts]
    hidden_ref = refs[2 * blocks + 1 + parts]
    width, middle = up_ref.shape
    rows = tokens[0].shape[0]
    x = jnp.concatenate([t[:, :width] for t in tokens], axis=0)
    table = jnp.concatenate([t[:, width:] for t in tokens], axis=0).astype(jnp.float32)
    here = lax.broadcasted_iota(jnp.int32, table.shape, 1) == mine_ref[0]
    scale = jnp.sum(jnp.where(here, table, 0.0), axis=1, keepdims=True)
    step = step_of(middle, 256)
    for j in range(0, middle, step):
        up = jnp.dot(x, up_ref[:, j:j + step], preferred_element_type=jnp.float32)
        hidden_ref[:, j:j + step] = (up / (1.0 + jnp.exp(-up))).astype(jnp.bfloat16)
    hidden = hidden_ref[...]
    at = 0
    for down_ref in downs:
        step = step_of(down_ref.shape[1], 512)
        for j in range(0, down_ref.shape[1], step):
            answer = jnp.dot(hidden, down_ref[:, j:j + step], preferred_element_type=jnp.float32)
            answer = answer.astype(jnp.bfloat16).astype(jnp.float32) * scale
            for i in range(blocks):
                outs[i][:, at:at + step] = answer[i * rows:(i + 1) * rows].astype(outs[i].dtype)
            at += step


def expert(mine, blocks, kept, up, down):
    rows = blocks[0].shape[0]
    width, middle = up.shape
    total = rows * len(blocks)
    vmem = pl.BlockSpec(memory_space=pltpu.VMEM)
    return pl.pallas_call(
        functools.partial(expert_body, len(blocks), len(down)),
        out_shape=[
            jax.ShapeDtypeStruct((rows, width), jnp.float32 if k else jnp.bfloat16) for k in kept
        ],
        in_specs=[pl.BlockSpec(memory_space=pltpu.SMEM)] + [vmem] * (len(blocks) + 1 + len(down)),
        out_specs=[vmem] * len(blocks),
        scratch_shapes=[pltpu.VMEM((total, middle), jnp.bfloat16)],
        compiler_params=pltpu.CompilerParams(vmem_limit_bytes=16 * 2**20),
        cost_estimate=pl.CostEstimate(
            flops=4 * total * width * middle, bytes_accessed=4 * width * middle, transcendentals=total * middle
        ),
    )(mine, *blocks, up, *down)


def load_body(first, pieces, source, out, sems):
    height, columns = out.shape[0] // pieces, out.shape[1]
    copies = []
    for i in range(pieces):
        s = pl.ds(i * height, height)
        copies.append(pltpu.make_async_copy(source.at[s, pl.ds(first, columns)], out.at[s], sems.at[i]))
        copies[-1].start()
    for c in copies:
        c.wait()


def load(matrix, first, last, after):
    matrix, _ = lax.optimization_barrier((matrix, after))
    height = matrix.shape[0]
    pieces = 8 if height % (8 * 16) == 0 else 1
    return pl.pallas_call(
        functools.partial(load_body, first, pieces),
        out_shape=pltpu.VMEM((height, last - first), matrix.dtype),
        in_specs=[pl.BlockSpec(memory_space=pltpu.HBM)],
        out_specs=pl.BlockSpec(memory_space=pltpu.VMEM),
        scratch_shapes=[pltpu.SemaphoreType.DMA((pieces,))],
        compiler_params=pltpu.CompilerParams(vmem_limit_bytes=16 * 2**20),
    )(pltpu.with_memory_space_constraint(matrix, pltpu.HBM))


def label_body(tokens_ref, ids_ref, weights_ref, out_ref):
    rows, width = tokens_ref.shape
    columns = out_ref.shape[1] - width
    expert_of = lax.broadcasted_iota(jnp.int32, (columns, rows), 0)
    weights = weights_ref[...].astype(jnp.float32)
    table = jnp.zeros((columns, rows), jnp.float32)
    for k in range(ids_ref.shape[0]):
        table = jnp.where(ids_ref[k:k + 1, :] == expert_of, weights[k:k + 1, :], table)
    one = lax.broadcasted_iota(jnp.int32, (rows, rows), 0) == lax.broadcasted_iota(jnp.int32, (rows, rows), 1)
    turned = lax.dot_general(
        one.astype(jnp.bfloat16),
        table.astype(jnp.bfloat16),
        (((1,), (1,)), ((), ())),
        preferred_element_type=jnp.float32,
    )
    out_ref[:, :width] = tokens_ref[...]
    out_ref[:, width:] = turned.astype(jnp.bfloat16)


def label(tokens, expert_ids, route_weights, columns):
    rows, width = tokens.shape
    vmem = pl.BlockSpec(memory_space=pltpu.VMEM)
    return pl.pallas_call(
        label_body,
        out_shape=pltpu.VMEM((rows, width + columns), jnp.bfloat16),
        in_specs=[vmem] * 3,
        out_specs=vmem,
    )(tokens, expert_ids.T, route_weights.T)


def ring_plan(tokens, expert_ids, route_weights, w_up, w_down):
    rows, width = tokens.shape
    experts = lax.axis_size(BOTH)
    n = lax.axis_size("local")
    half = n // 2
    mine = lax.axis_index(BOTH).astype(jnp.int32)[None]
    order = list(range(0, n, 2)) + list(range(n - 1, 0, -2))
    onward = [(order[i], order[(i + 1) % n]) for i in range(n)]
    pairs = onward + [(n + b, n + a) for a, b in onward]
    def hop(x):
        return lax.ppermute(x, BOTH, pairs)

    def swap(x):
        return lax.ppermute(x, "node", [(0, 1), (1, 0)])

    def bf(x):
        return x.astype(jnp.bfloat16)

    columns = -(-experts // LANES) * LANES
    own = label(tokens, expert_ids, route_weights, columns)

    a, b = [own], [swap(own)]
    ahead_a, ahead_b = [None], [None]
    behind, ahead = {}, {}

    def compute(h, first=None):
        blocks = (a[h], b[h], ahead_a[h], ahead_b[h])
        if first is not None:
            blocks, _ = lax.optimization_barrier((blocks, first))
        r = expert(mine, blocks, (False, False, True, True), up, down)
        behind[h], ahead[h] = r[:2], r[2:]

    step = step_of(width, 512)
    cut = (width // step * LATE[0] // LATE[1]) * step
    up, mine = lax.optimization_barrier((load(w_up[0], 0, w_up.shape[2], b[0]), mine))
    for h in range(1, half + 1):
        a.append(hop(a[-1]))
        if h < half:
            b.append(hop(b[-1]))
        if h == 1:
            a[1], up = lax.optimization_barrier((a[1], up))
            up = pltpu.with_memory_space_constraint(up, pltpu.VMEM)
        elif h == 2:
            down = load(w_down[0], 0, cut, a[1])
            a[2], down_first = lax.optimization_barrier((a[2], down))
        elif h == 3:
            down = load(w_down[0], cut, width, (a[2], ahead_b[2]))
            a[3], down_last = lax.optimization_barrier((a[3], down))
        if 1 < h < half:
            a[h], ahead_a[h - 1], ahead_b[h - 1] = lax.optimization_barrier((a[h], ahead_a[h - 1], ahead_b[h - 1]))
        if h < half:
            ahead_b.append(swap(a[h]))
            ahead_a.append(swap(b[h]))
    down = [pltpu.with_memory_space_constraint(d, pltpu.VMEM) for d in (down_first, down_last)]
    near, h = range(1, half - 2), half - 1
    blocks = [a[h], ahead_b[h]]
    for i in near:
        blocks += [a[i], b[i], ahead_a[i], ahead_b[i]]
    r = expert(mine, blocks, (False, True) + (False, False, True, True) * len(near), up, down)
    r, a[half] = lax.optimization_barrier((r, a[half]))
    for i in near:
        behind[i], ahead[i] = r[4 * i - 2:4 * i], r[4 * i:4 * i + 2]
    ahead_b.append(swap(a[half]))
    last = expert(mine, (b[h], ahead_a[h], a[half], ahead_b[half]), (False, True, True, False), up, down)
    behind[h], ahead[h], far = (r[0], last[0]), (last[1], r[1]), last[2:]

    def join(x, y):
        return x.astype(jnp.float32) + y.astype(jnp.float32)

    def total(h, after=None):
        mine_a, mine_b = behind[h]
        if after is not None:
            mine_a, mine_b, _ = lax.optimization_barrier((mine_a, mine_b, after))
        sum_b = join(ahead[h][1], swap(mine_a))
        return [join(ahead[h][0], swap(mine_b)), sum_b]

    send_a = bf(join(far[0], swap(far[1])))
    sums = {half - 1: total(half - 1)}
    send_b = bf(sums[half - 1][1])
    run_a = hop(send_a)
    run_b = hop(send_b)
    compute(half - 2, (send_a, send_b))
    sums[half - 2] = total(half - 2)
    for h in range(half - 1, 0, -1):
        if h < half - 1:
            run_b = hop(bf(join(sums[h][1], run_b)))
        send_a = bf(join(sums[h][0], run_a))
        if h - 1 > 0 and h - 1 not in sums:
            sums[h - 1] = total(h - 1, send_a)
        run_a = hop(send_a)
    blocks, _ = lax.optimization_barrier(((a[0], b[0]), send_a))
    own_a, own_b = expert(mine, blocks, (True, True), up, down)
    last = swap(bf(join(own_b, run_b)))
    return bf(join(join(own_a, run_a), last))


def solution(mesh):
    placed = (
        P(("rep", "node", "local"), None),
        P(("rep", "node", "local"), None),
        P(("rep", "node", "local"), None),
        P(("node", "local"), None, None),
        P(("node", "local"), None, None),
    )
    n = mesh.shape["local"]
    ringed = mesh.shape["node"] == 2 and n % 2 == 0 and 6 <= n <= 16
    return jax.shard_map(
        ring_plan if ringed else gather_plan,
        mesh=mesh,
        in_specs=placed,
        out_specs=P(("rep", "node", "local"), None),
        check_vma=False,
    )
```
